256 devices in a mesh: seq: 64 (over y, z_lo, x), tensor: 4 (over z_hi, core).
Axes of the slice: x: 4, y: 4, z: 8 (z_hi: 2, z_lo: 4; z = z_hi * 4 + z_lo), core: 2. Of those that a mesh axis runs over, the one named last changes fastest.
Arguments:
- queries: bfloat16 [32768, 3072], P('seq', 'tensor'), may hold values from -180 to 180, as said below
- ref_keys: bfloat16 [1024, 3072], P('seq', 'tensor'), may hold values from -6 to 6
- ref_values: bfloat16 [1024, 3072], P('seq', 'tensor'), may hold values from -6 to 6
- grad_out: bfloat16 [32768, 3072], P('seq', 'tensor'), may hold values from -12 to 12
- key_weight: bfloat16 [3072, 3072], P(None, 'tensor'), may hold values from -0.109375 to 0.109375
- value_weight: bfloat16 [3072, 3072], P(None, 'tensor'), may hold values from -0.109375 to 0.109375
Outputs:
- grad_queries: bfloat16 [32768, 3072], P('seq', 'tensor')
- grad_ref_rows: bfloat16 [1024, 3072], P('seq', 'tensor')
The draws below stay inside these ranges and needn't reach their ends.
Inputs may be any that keep to these rules, and one draw needn't show every extreme that they name: `queries`: queries of order one, some rows larger.
All inputs are finite; a program needn't handle non-finite values.
Results may differ from the reference program's by a relative error of at most 0.015.
Values may be sent and summed in bfloat16 or wider, within the bound.
No kernel may reach another device: no remote copies, remote signals or barrier semaphores. Data moves between devices by JAX's collectives and lax.ppermute only.
A program may use at most 128 MiB of HBM per device.

```python
import jax
import jax.numpy as jnp
from jax import lax

D = 3072
HEADS = 24
HD = 128
TOK_DEV = 512
TOKENS = 32768
REF = 1024
N_SEQ = 64


def key_rows(key):
    return jnp.clip(jax.random.normal(jax.random.fold_in(key, 11), (REF, D), jnp.float32), -6.0, 6.0)


def draw_ref_keys(key, part):
    return key_rows(key).astype(jnp.bfloat16)


def draw_queries(key, part):
    base = jnp.clip(jax.random.normal(jax.random.fold_in(key, 23), (TOKENS, D), jnp.float32), -6.0, 6.0)
    return base.astype(jnp.bfloat16)


def level_of(key, extent, split, smallest, top_value):
    def one(axis_at, blocks):
        heights = jax.random.uniform(jax.random.fold_in(jax.random.fold_in(key, 6), axis_at), (blocks,), jnp.float32, smallest / len(split), top_value / len(split))
        return jnp.repeat(jnp.exp(heights), extent[axis_at] // blocks).reshape((-1,) + (1,) * (len(extent) - axis_at - 1))

    gain = one(*split[0])
    for cut in split[1:]:
        gain = gain * one(*cut)
    return gain


def scatter_about(stream_key, extent, deviation, reach, cuts=(), held_as=jnp.bfloat16):
    entries = deviation * jax.random.normal(stream_key, extent, jnp.float32)
    if cuts:
        entries = entries * level_of(stream_key, extent, cuts, -0.22, 0.18)
    return jnp.clip(entries, -reach, reach).astype(held_as)


def setup_inputs(seed: int = 0) -> dict:
    splits = jax.random.split(jax.random.key(seed), 7)
    queries = draw_queries(jax.random.fold_in(splits[6], 71), 0)
    ref_keys = draw_ref_keys(jax.random.fold_in(splits[6], 71), 0)
    ref_values = scatter_about(splits[2], (REF, D), 1.0, 6.0, ((0, 64), (1, 4)))
    grad_out = scatter_about(splits[3], (TOKENS, D), 2.0, 12.0, ((0, 64), (1, 4)))
    key_weight = scatter_about(splits[4], (D, D), D ** -0.5, 0.109375, ((1, 4),))
    value_weight = scatter_about(splits[5], (D, D), D ** -0.5, 0.109375, ((1, 4),))
    return {"queries": queries, "ref_keys": ref_keys, "ref_values": ref_values, "grad_out": grad_out, "key_weight": key_weight, "value_weight": value_weight}


def head_grads(pieces):
    query_h, key_h, value_h, grad_h = pieces
    scale = 1.0 / (HD ** 0.5)
    scores = jnp.dot(query_h, key_h.T, preferred_element_type=jnp.float32) * scale
    probs = jax.nn.softmax(scores, axis=-1)
    probs_b = probs.astype(jnp.bfloat16)
    grad_probs = jnp.dot(grad_h, value_h.T, preferred_element_type=jnp.float32)
    delta = jnp.sum(probs * grad_probs, axis=-1, keepdims=True)
    grad_scores = (probs * (grad_probs - delta)).astype(jnp.bfloat16)
    grad_query = (jnp.dot(grad_scores, key_h, preferred_element_type=jnp.float32) * scale).astype(jnp.bfloat16)
    score_blocks = grad_scores.astype(jnp.float32).reshape(N_SEQ, TOK_DEV, REF)
    prob_blocks = probs_b.astype(jnp.float32).reshape(N_SEQ, TOK_DEV, REF)
    query_blocks = query_h.astype(jnp.float32).reshape(N_SEQ, TOK_DEV, HD)
    grad_blocks = grad_h.astype(jnp.float32).reshape(N_SEQ, TOK_DEV, HD)
    key_parts = (jnp.einsum("str,std->srd", score_blocks, query_blocks) * scale).astype(jnp.bfloat16)
    value_parts = jnp.einsum("str,std->srd", prob_blocks, grad_blocks).astype(jnp.bfloat16)
    key_parts, value_parts = lax.optimization_barrier((key_parts, value_parts))
    grad_key = jnp.sum(key_parts.astype(jnp.float32), axis=0)
    grad_value = jnp.sum(value_parts.astype(jnp.float32), axis=0)
    return grad_query, grad_key, grad_value


def split_heads(matrix):
    return jnp.transpose(matrix.reshape(matrix.shape[0], HEADS, HD), (1, 0, 2))


def join_heads(stacked):
    return jnp.transpose(stacked, (1, 0, 2)).reshape(stacked.shape[1], HEADS * HD)


def reference(queries, ref_keys, ref_values, grad_out, key_weight, value_weight):
    grad_query, grad_key, grad_value = lax.map(head_grads, (split_heads(queries), split_heads(ref_keys), split_heads(ref_values), split_heads(grad_out)))
    grad_queries = join_heads(grad_query)
    key_sums = join_heads(grad_key)
    value_sums = join_heads(grad_value)
    rows = jnp.dot(key_sums, key_weight.astype(jnp.float32).T, precision=lax.Precision.HIGHEST, preferred_element_type=jnp.float32)
    rows = rows + jnp.dot(value_sums, value_weight.astype(jnp.float32).T, precision=lax.Precision.HIGHEST, preferred_element_type=jnp.float32)
    return grad_queries, rows.astype(jnp.bfloat16)
```

```python
import functools
import math

import jax
import jax.numpy as jnp
from jax import lax
from jax.experimental import pallas as pl
from jax.experimental.pallas import tpu as pltpu
from jax.sharding import PartitionSpec as P

HD = 128
SCALE = 1.0 / HD**0.5
NN = (((1,), (0,)), ((), ()))
NT = (((1,), (1,)), ((), ()))
TN = (((0,), (0,)), ((), ()))

SIDE = 4
CORES = 2
TENSOR = 4
BOTH = ("seq", "tensor")


def dot(a, b, dims=NN):
    return lax.dot_general(a, b, dims, preferred_element_type=jnp.float32)


def ring_pairs(axes, step):
    pairs = []
    for y in range(SIDE):
        for z in range(SIDE):
            for x in range(SIDE):
                for t in range(TENSOR):
                    place = {"y": y, "z": z, "x": x}
                    to = dict(place)
                    along = axes[t % CORES]
                    to[along] = (place[along] + step) % SIDE
                    pairs.append(
                        tuple(
                            ((p["y"] * SIDE + p["z"]) * SIDE + p["x"]) * TENSOR + t
                            for p in (place, to)
                        )
                    )
    return pairs


def ring_send(block, axes, step):
    return lax.ppermute(block, BOTH, ring_pairs(axes, step))


def flip_send(block, flip):
    pairs = [(i, i ^ flip) for i in range(SIDE**3 * TENSOR)]
    return lax.ppermute(block, BOTH, pairs)


STEPS = (1, 3, 2)


def gather(block, axes):
    return [block] + [ring_send(block, axes, step) for step in STEPS]


def scatter(blocks, axes):
    back = [(SIDE - step) % SIDE for step in STEPS]
    return [ring_send(block, axes, step) for block, step in zip(blocks[1:], back)]


def attention_kernel(chunk, q_ref, g_ref, *refs):
    keys, values = refs[0:SIDE], refs[SIDE : 2 * SIDE]
    dq_ref, parts = refs[2 * SIDE], refs[2 * SIDE + 1 : 3 * SIDE + 1]
    probs_ref, grads_ref = refs[3 * SIDE + 1 :]
    rows = keys[0].shape[0]
    tokens = q_ref.shape[0]
    for at in range(0, tokens, chunk):
        some = pl.ds(at, chunk)
        q, g = q_ref[some, :], g_ref[some, :]
        scores = [dot(k[...], q, NT) for k in keys]
        top = functools.reduce(
            jnp.maximum, [jnp.max(s, axis=0, keepdims=True) for s in scores]
        )
        raised = [jnp.exp2((s - top) * (SCALE * math.log2(math.e))) for s in scores]
        inverse = 1.0 / sum(jnp.sum(e, axis=0, keepdims=True) for e in raised)
        probs = [e * inverse for e in raised]
        grad_probs = [dot(v[...], g, NT) for v in values]
        delta = sum(
            jnp.sum(p * d, axis=0, keepdims=True) for p, d in zip(probs, grad_probs)
        )
        for i, (p, d) in enumerate(zip(probs, grad_probs)):
            here = pl.ds(i * rows, rows)
            probs_ref[here, some] = p.astype(jnp.bfloat16)
            grads_ref[here, some] = (p * (d - delta)).astype(jnp.bfloat16)
    q, g = q_ref[...], g_ref[...]
    dq = jnp.zeros((HD, tokens), jnp.float32)
    for i in range(SIDE):
        here = pl.ds(i * rows, rows)
        grads = grads_ref[here, :]
        parts[i][:, :HD] = (dot(grads, q) * SCALE).astype(jnp.bfloat16)
        parts[i][:, HD:] = dot(probs_ref[here, :], g).astype(jnp.bfloat16)
        dq += dot(keys[i][...], grads, TN)
    dq_ref[...] = (dq.T * SCALE).astype(jnp.bfloat16)


def attention(queries, grad_out, blocks):
    tokens, width = queries.shape
    heads = width // HD
    rows = blocks[0].shape[0]
    token_spec = pl.BlockSpec((tokens, HD), lambda h: (0, h))
    key_spec = pl.BlockSpec((rows, HD), lambda h: (0, h))
    value_spec = pl.BlockSpec((rows, HD), lambda h: (0, heads + h))
    part_spec = pl.BlockSpec((rows, 2 * HD), lambda h: (0, h))
    return pl.pallas_call(
        functools.partial(attention_kernel, tokens // 2),
        grid=(heads,),
        in_specs=[token_spec] * 2 + [key_spec] * SIDE + [value_spec] * SIDE,
        out_specs=[token_spec] + [part_spec] * SIDE,
        out_shape=[jax.ShapeDtypeStruct(queries.shape, jnp.bfloat16)]
        + [jax.ShapeDtypeStruct((rows, 2 * width), jnp.bfloat16)] * SIDE,
        scratch_shapes=[pltpu.VMEM((SIDE * rows, tokens), jnp.bfloat16)] * 2,
        compiler_params=pltpu.CompilerParams(vmem_limit_bytes=32 * 2**20),
        name="attention_grads",
    )(queries, grad_out, *blocks, *blocks)


def project_kernel(own_ref, a_ref, b_ref, c_ref, key_ref, value_ref, out_ref):
    total = own_ref[...]
    for ref in (a_ref, b_ref, c_ref):
        total += ref[...].astype(jnp.float32)
    rows, width = total.shape
    high = total.astype(jnp.bfloat16)
    low = (total - high.astype(jnp.float32)).astype(jnp.bfloat16)
    both = jnp.concatenate([high, low], axis=0)
    pieces = [both[:, at : at + HD] for at in range(0, width, HD)]
    result = dot(jnp.concatenate(pieces[0::2], axis=1), key_ref[...], NT)
    result += dot(jnp.concatenate(pieces[1::2], axis=1), value_ref[...], NT)
    out_ref[...] = (result[:rows] + result[rows:]).astype(jnp.bfloat16)


def project(own, received, key_weight, value_weight):
    rows, width = own.shape
    features, columns = key_weight.shape
    block = 512
    sum_spec = pl.BlockSpec((rows, width), lambda n: (0, 0))
    weight_spec = pl.BlockSpec((block, columns), lambda n: (n, 0))
    return pl.pallas_call(
        project_kernel,
        grid=(features // block,),
        in_specs=[sum_spec] * 4 + [weight_spec] * 2,
        out_specs=pl.BlockSpec((rows, block), lambda n: (0, n)),
        out_shape=jax.ShapeDtypeStruct((rows, features), jnp.bfloat16),
        compiler_params=pltpu.CompilerParams(vmem_limit_bytes=16 * 2**20),
        name="project_rows",
    )(own, *received, key_weight, value_weight)


def shards(queries, ref_keys, ref_values, grad_out, key_weight, value_weight):
    rows = jnp.concatenate([ref_keys, ref_values], axis=1)
    rows = jnp.concatenate(gather(rows, ("z", "z")), axis=0)
    rows = jnp.concatenate(gather(rows, ("x", "y")), axis=0)
    blocks = gather(rows, ("y", "x"))

    grad_queries, *parts = attention(queries, grad_out, blocks)

    total = parts[0].astype(jnp.float32)
    received = scatter(parts, ("y", "x"))
    for axes in (("x", "y"), ("z", "z")):
        for r in received:
            total += r.astype(jnp.float32)
        cut = jnp.split(total, SIDE, axis=0)
        total = cut[0]
        received = scatter([c.astype(jnp.bfloat16) for c in cut], axes)
    result = project(total, received, key_weight, value_weight)

    columns = result.shape[1] // TENSOR
    me = lax.axis_index("tensor")

    def block_of(flip):
        return lax.dynamic_slice_in_dim(result, (me ^ flip) * columns, columns, axis=1)

    grad_rows = block_of(0).astype(jnp.float32)
    for r in [flip_send(block_of(flip), flip) for flip in (1, 2, 3)]:
        grad_rows += r.astype(jnp.float32)
    return grad_queries, grad_rows.astype(jnp.bfloat16)


def solution(mesh):
    placed = (
        P("seq", "tensor"),
        P("seq", "tensor"),
        P("seq", "tensor"),
        P("seq", "tensor"),
        P(None, "tensor"),
        P(None, "tensor"),
    )
    return jax.shard_map(
        shards,
        mesh=mesh,
        in_specs=placed,
        out_specs=(P("seq", "tensor"), P("seq", "tensor")),
        check_vma=False,
    )
```

```python
import functools
import math

import jax
import jax.numpy as jnp
from jax import lax
from jax.experimental import pallas as pl
from jax.experimental.pallas import tpu as pltpu
from jax.sharding import PartitionSpec as P

HD = 128
SCALE = 1.0 / HD**0.5
NN = (((1,), (0,)), ((), ()))
NT = (((1,), (1,)), ((), ()))
TN = (((0,), (0,)), ((), ()))

SIDE = 4
CORES = 2
TENSOR = 4
BOTH = ("seq", "tensor")


def dot(a, b, dims=NN):
    return lax.dot_general(a, b, dims, preferred_element_type=jnp.float32)


def ring_pairs(axes, step):
    pairs = []
    for y in range(SIDE):
        for z in range(SIDE):
            for x in range(SIDE):
                for t in range(TENSOR):
                    place = {"y": y, "z": z, "x": x}
                    to = dict(place)
                    along = axes[t % CORES]
                    to[along] = (place[along] + step) % SIDE
                    pairs.append(
                        tuple(
                            ((p["y"] * SIDE + p["z"]) * SIDE + p["x"]) * TENSOR + t
                            for p in (place, to)
                        )
                    )
    return pairs


def ring_send(block, axes, step):
    return lax.ppermute(block, BOTH, ring_pairs(axes, step))


def flip_send(block, flip):
    pairs = [(i, i ^ flip) for i in range(SIDE**3 * TENSOR)]
    return lax.ppermute(block, BOTH, pairs)


STEPS = (1, 3, 2)


def gather(block, axes):
    return [block] + [ring_send(block, axes, step) for step in STEPS]


def scatter(blocks, axes):
    back = [(SIDE - step) % SIDE for step in STEPS]
    return [ring_send(block, axes, step) for block, step in zip(blocks[1:], back)]


def attention_kernel(chunk, q_ref, g_ref, *refs):
    keys, values = refs[0:SIDE], refs[SIDE : 2 * SIDE]
    *_, probs_ref, grads_ref = refs
    dq_ref, parts = refs[-SIDE - 3], refs[-SIDE - 2 : -2]
    rows = keys[0].shape[0]
    tokens = q_ref.shape[0]
    for at in range(0, tokens, chunk):
        some = pl.ds(at, chunk)
        q, g = q_ref[some, :], g_ref[some, :]
        scores = [dot(k[...], q, NT) for k in keys]
        top = functools.reduce(
            jnp.maximum, [jnp.max(s, axis=0, keepdims=True) for s in scores]
        )
        raised = [jnp.exp2((s - top) * (SCALE * math.log2(math.e))) for s in scores]
        inverse = 1.0 / sum(jnp.sum(e, axis=0, keepdims=True) for e in raised)
        probs = [e * inverse for e in raised]
        grad_probs = [dot(v[...], g, NT) for v in values]
        delta = sum(
            jnp.sum(p * d, axis=0, keepdims=True) for p, d in zip(probs, grad_probs)
        )
        for i, (p, d) in enumerate(zip(probs, grad_probs)):
            here = pl.ds(i * rows, rows)
            probs_ref[here, some] = p.astype(jnp.bfloat16)
            grads_ref[here, some] = (p * (d - delta)).astype(jnp.bfloat16)
    q, g = q_ref[...], g_ref[...]
    dq = jnp.zeros((HD, tokens), jnp.float32)
    for i in range(SIDE):
        here = pl.ds(i * rows, rows)
        grads = grads_ref[here, :]
        parts[i][:, :HD] = (dot(grads, q) * SCALE).astype(jnp.bfloat16)
        parts[i][:, HD:] = dot(probs_ref[here, :], g).astype(jnp.bfloat16)
        dq += dot(keys[i][...], grads, TN)
    dq_ref[...] = (dq.T * SCALE).astype(jnp.bfloat16)


def attention(queries, grad_out, blocks, first, grad_queries=None):
    tokens, width = queries.shape
    rows, columns = blocks[0].shape
    heads = columns // (2 * HD)
    token_spec = pl.BlockSpec((tokens, HD), lambda h: (0, first + h))
    key_spec = pl.BlockSpec((rows, HD), lambda h: (0, h))
    value_spec = pl.BlockSpec((rows, HD), lambda h: (0, heads + h))
    part_spec = pl.BlockSpec((rows, 2 * HD), lambda h: (0, h))
    operands = [queries, grad_out, *blocks, *blocks]
    in_specs = [token_spec] * 2 + [key_spec] * SIDE + [value_spec] * SIDE
    aliases = {}
    if grad_queries is not None:
        aliases = {len(operands): 0}
        operands.append(grad_queries)
        in_specs.append(pl.BlockSpec(memory_space=pl.ANY))
    scores = heads * tokens * SIDE * rows
    return pl.pallas_call(
        functools.partial(attention_kernel, tokens // 2),
        grid=(heads,),
        in_specs=in_specs,
        out_specs=[token_spec] + [part_spec] * SIDE,
        out_shape=[jax.ShapeDtypeStruct(queries.shape, jnp.bfloat16)]
        + [jax.ShapeDtypeStruct((rows, columns), jnp.bfloat16)] * SIDE,
        scratch_shapes=[pltpu.VMEM((SIDE * rows, tokens), jnp.bfloat16)] * 2,
        input_output_aliases=aliases,
        compiler_params=pltpu.CompilerParams(vmem_limit_bytes=24 * 2**20),
        cost_estimate=pl.CostEstimate(
            flops=10 * HD * scores,
            bytes_accessed=2 * (3 * tokens * heads * HD + 2 * SIDE * rows * columns),
            transcendentals=scores,
        ),
        name="attention_grads",
    )(*operands)


def project_kernel(own_ref, a_ref, b_ref, c_ref, key_ref, value_ref, out_ref):
    total = own_ref[...]
    for ref in (a_ref, b_ref, c_ref):
        total += ref[...].astype(jnp.float32)
    rows, width = total.shape
    high = total.astype(jnp.bfloat16)
    low = (total - high.astype(jnp.float32)).astype(jnp.bfloat16)
    both = jnp.concatenate([high, low], axis=0)
    pieces = [both[:, at : at + HD] for at in range(0, width, HD)]
    result = dot(jnp.concatenate(pieces[0::2], axis=1), key_ref[...], NT)
    result += dot(jnp.concatenate(pieces[1::2], axis=1), value_ref[...], NT)
    out_ref[...] = (result[:rows] + result[rows:]).astype(jnp.bfloat16)


def project(own, received, key_weight, value_weight):
    rows, width = own.shape
    features, columns = key_weight.shape
    block = 512
    sum_spec = pl.BlockSpec((rows, width), lambda n: (0, 0))
    weight_spec = pl.BlockSpec((block, columns), lambda n: (n, 0))
    return pl.pallas_call(
        project_kernel,
        grid=(features // block,),
        in_specs=[sum_spec] * 4 + [weight_spec] * 2,
        out_specs=pl.BlockSpec((rows, block), lambda n: (0, n)),
        out_shape=jax.ShapeDtypeStruct((rows, features), jnp.bfloat16),
        compiler_params=pltpu.CompilerParams(vmem_limit_bytes=52 * 2**20),
        name="project_rows",
    )(own, *received, key_weight, value_weight)


def shards(queries, ref_keys, ref_values, grad_out, key_weight, value_weight):
    groups = 2
    heads = queries.shape[1] // HD // groups
    width = heads * HD
    cuts = [slice(i * width, (i + 1) * width) for i in range(groups)]
    rows = jnp.concatenate([a[:, c] for c in cuts for a in (ref_keys, ref_values)], axis=1)
    rows = jnp.concatenate(gather(rows, ("z", "z")), axis=0)
    pieces = gather(rows, ("x", "y"))
    rows = [
        jnp.concatenate([p[:, 2 * c.start : 2 * c.stop] for p in pieces], axis=0) for c in cuts
    ]
    blocks = [gather(r, ("y", "x")) for r in rows]

    grad_queries, totals = None, []
    for i in range(groups):
        grad_queries, *parts = attention(queries, grad_out, blocks[i], i * heads, grad_queries)
        total = parts[0].astype(jnp.float32)
        for r in scatter(parts, ("y", "x")):
            total += r.astype(jnp.float32)
        totals.append(total)
    total = jnp.concatenate(totals, axis=1)
    for axes in (("x", "y"), ("z", "z")):
        cut = jnp.split(total, SIDE, axis=0)
        received = scatter([c.astype(jnp.bfloat16) for c in cut], axes)
        if axes == ("z", "z"):
            break
        total = cut[0]
        for r in received:
            total += r.astype(jnp.float32)
    result = project(cut[0], received, key_weight, value_weight)

    me = lax.axis_index("tensor")
    half, core = me // CORES, me % CORES
    columns = result.shape[1] // TENSOR

    def blocks_of(array, index):
        return jnp.concatenate(
            [
                lax.dynamic_slice_in_dim(array, (h * CORES + index) * columns, columns, axis=1)
                for h in range(TENSOR // CORES)
            ],
            axis=1,
        )

    pair = flip_send(blocks_of(result, 1 - core), 1).astype(jnp.float32)
    pair += blocks_of(result, core).astype(jnp.float32)
    away = lax.dynamic_slice_in_dim(pair, (1 - half) * columns, columns, axis=1)
    here = lax.dynamic_slice_in_dim(pair, half * columns, columns, axis=1)
    grad_rows = here + flip_send(away.astype(jnp.bfloat16), CORES).astype(jnp.float32)
    return grad_queries, grad_rows.astype(jnp.bfloat16)


def solution(mesh):
    placed = (
        P("seq", "tensor"),
        P("seq", "tensor"),
        P("seq", "tensor"),
        P("seq", "tensor"),
        P(None, "tensor"),
        P(None, "tensor"),
    )
    return jax.shard_map(
        shards,
        mesh=mesh,
        in_specs=placed,
        out_specs=(P("seq", "tensor"), P("seq", "tensor")),
        check_vma=False,
    )
```

```python
import functools
import math

import jax
import jax.numpy as jnp
from jax import lax
from jax.experimental import pallas as pl
from jax.experimental.pallas import tpu as pltpu
from jax.sharding import PartitionSpec as P

HD = 128
SCALE = 1.0 / HD**0.5
NN = (((1,), (0,)), ((), ()))
NT = (((1,), (1,)), ((), ()))
TN = (((0,), (0,)), ((), ()))

DEVICES = 256
Y, Z, X, HALF, CORE = 64, 16, 4, 2, 1
LATE = (X, Y)
EARLY = (Y, X)
STEPS = (1, 3, 2)


def swap(block, axes, step=1):
    pairs = [(i, i ^ (step * axes[i % 2])) for i in range(DEVICES)]
    return lax.ppermute(block, ("seq", "tensor"), pairs)


def gather(block, axes):
    return [block] + [swap(block, axes, step) for step in STEPS]


def scatter_sum(blocks, axes):
    total = wide(blocks[0])
    for block, step in zip(blocks[1:], STEPS):
        total += wide(swap(narrow(block), axes, step))
    return total


def wide(array):
    return array.astype(jnp.float32)


def narrow(array):
    return array.astype(jnp.bfloat16)


def dot(a, b, dims=NN):
    return lax.dot_general(a, b, dims, preferred_element_type=jnp.float32)


def join(*rows):
    return jnp.concatenate(rows, axis=0)


def attention_kernel(chunk, parity_ref, *refs):
    queries, grads_out = (refs[0], refs[2]), (refs[1], refs[3])
    keys, values = refs[4:8], refs[8:12]
    grad_queries, parts = refs[12:14], refs[14:18]
    probs_ref, grads_ref = refs[18:]
    rows = keys[0].shape[0]
    tokens = queries[0].shape[0]
    for n in range(2):
        for at in range(0, tokens, chunk):
            q, g = queries[n][pl.ds(at, chunk), :], grads_out[n][pl.ds(at, chunk), :]
            some = pl.ds(n * tokens + at, chunk)
            scores = [dot(k[...], q, NT) for k in keys]
            top = functools.reduce(
                jnp.maximum, [jnp.max(s, axis=0, keepdims=True) for s in scores]
            )
            raised = [jnp.exp2((s - top) * (SCALE * math.log2(math.e))) for s in scores]
            inverse = 1.0 / sum(jnp.sum(e, axis=0, keepdims=True) for e in raised)
            probs = [e * inverse for e in raised]
            grad_probs = [dot(v[...], g, NT) for v in values]
            delta = sum(
                jnp.sum(p * d, axis=0, keepdims=True) for p, d in zip(probs, grad_probs)
            )
            for i, (p, d) in enumerate(zip(probs, grad_probs)):
                here = pl.ds(i * rows, rows)
                probs_ref[here, some] = narrow(p)
                grads_ref[here, some] = narrow(p * (d - delta))
    spans = [pl.ds(n * tokens, tokens) for n in range(2)]
    for i in range(4):
        here = pl.ds(i * rows, rows)
        dk = sum(dot(grads_ref[here, t], q[...]) for t, q in zip(spans, queries))
        dv = sum(dot(probs_ref[here, t], g[...]) for t, g in zip(spans, grads_out))
        parts[i][:, :HD] = narrow(dk * SCALE)
        parts[i][:, HD:] = narrow(dv)
    for t, out_ref in zip(spans, grad_queries):
        dq = sum(dot(k[...], grads_ref[pl.ds(i * rows, rows), t], TN) for i, k in enumerate(keys))
        out_ref[...] = narrow(dq.T * SCALE)


def attention(parity, queries, grad_out, far, blocks, result_shape):
    tokens, width = queries.shape
    rows, columns = blocks[0].shape
    heads = width // HD
    placed = pl.BlockSpec((tokens, HD), lambda h, parity: (0, parity[0] * heads + h))
    token = pl.BlockSpec((tokens, HD), lambda h, parity: (0, h))
    token_second = pl.BlockSpec((tokens, HD), lambda h, parity: (0, heads + h))
    key = pl.BlockSpec((rows, HD), lambda h, parity: (0, h))
    value = pl.BlockSpec((rows, HD), lambda h, parity: (0, heads + h))
    part = pl.BlockSpec((rows, 2 * HD), lambda h, parity: (0, h))
    scores = heads * 2 * tokens * 4 * rows
    shapes = [result_shape, queries.shape] + [b.shape for b in blocks]
    return pl.pallas_call(
        functools.partial(attention_kernel, tokens // 2),
        grid_spec=pltpu.PrefetchScalarGridSpec(
            num_scalar_prefetch=1,
            grid=(heads,),
            in_specs=[token] * 2 + [token, token_second] + [key] * 4 + [value] * 4,
            out_specs=[placed, token] + [part] * 4,
            scratch_shapes=[pltpu.VMEM((4 * rows, 2 * tokens), jnp.bfloat16)] * 2,
        ),
        out_shape=[jax.ShapeDtypeStruct(shape, jnp.bfloat16) for shape in shapes],
        compiler_params=pltpu.CompilerParams(vmem_limit_bytes=24 * 2**20),
        cost_estimate=pl.CostEstimate(
            flops=10 * HD * scores,
            bytes_accessed=2 * (6 * tokens * heads * HD + 8 * rows * columns),
            transcendentals=scores,
        ),
        name="attention_grads",
    )(parity, queries, grad_out, far, far, *blocks, *blocks)


def project_kernel(
    blocks,
    parity_ref,
    mine_ref,
    other_ref,
    key_ref,
    value_ref,
    far_ref,
    _,
    out_ref,
    near_ref,
    key_held,
    value_held,
    weight_sems,
    far_sem,
):
    features = key_ref.shape[0] // blocks
    copies = []
    for n in range(blocks):
        here = pl.ds(n * features, features)
        pairs = ((key_ref, key_held), (value_ref, value_held))
        copies.append(
            [
                pltpu.make_async_copy(a.at[here, :], b.at[here, :], weight_sems.at[i, n])
                for i, (a, b) in enumerate(pairs)
            ]
        )
        for copy in copies[-1]:
            copy.start()
    half = far_ref.shape[1]
    place = pl.ds(pl.multiple_of((1 - parity_ref[0]) * half, half), half)
    far_copy = pltpu.make_async_copy(far_ref, near_ref.at[:, place], far_sem)
    far_copy.start()

    def halves(sums):
        high = narrow(sums)
        return join(high, narrow(sums - wide(high)))

    rows, width = mine_ref.shape
    mine, other = halves(mine_ref[...]), halves(other_ref[...])
    first = parity_ref[0] == 0
    left = jnp.where(first, mine, other)
    right = jnp.where(first, other, mine)

    def both(start):
        picks = range(start, width, 2 * HD)
        return jnp.concatenate([a[:, at : at + HD] for a in (left, right) for at in picks], axis=1)

    keys, values = both(0), both(HD)
    for n in range(blocks):
        here = pl.ds(n * features, features)
        for copy in copies[n]:
            copy.wait()
        result = dot(keys, key_held[here, :], NT) + dot(values, value_held[here, :], NT)
        out_ref[:, here] = narrow(result[:rows] + result[rows:])
    far_copy.wait()


def project(parity, mine, other, key_weight, value_weight, grad_far, grad_queries):
    blocks = 6
    vmem = pl.BlockSpec(memory_space=pltpu.VMEM)
    whole = pl.BlockSpec(memory_space=pl.ANY)
    return pl.pallas_call(
        functools.partial(project_kernel, blocks),
        in_specs=[pl.BlockSpec(memory_space=pltpu.SMEM)] + [vmem] * 2 + [whole] * 4,
        out_specs=[vmem, whole],
        out_shape=[
            jax.ShapeDtypeStruct((mine.shape[0], key_weight.shape[0]), jnp.bfloat16),
            jax.ShapeDtypeStruct(grad_queries.shape, jnp.bfloat16),
        ],
        scratch_shapes=[pltpu.VMEM(key_weight.shape, jnp.bfloat16)] * 2
        + [pltpu.SemaphoreType.DMA((2, blocks)), pltpu.SemaphoreType.DMA],
        input_output_aliases={6: 1},
        compiler_params=pltpu.CompilerParams(vmem_limit_bytes=52 * 2**20),
        name="project_rows",
    )(parity, mine, other, key_weight, value_weight, grad_far, grad_queries)


def shards(queries, ref_keys, ref_values, grad_out, key_weight, value_weight):
    parity = lax.axis_index("seq") // (Z // X) % 2
    half = queries.shape[1] // 2

    def columns(array, which):
        return lax.dynamic_slice_in_dim(array, which * half, half, axis=1)

    mine = jnp.concatenate([columns(ref_keys, parity), columns(ref_values, parity)], axis=1)
    other = jnp.concatenate(
        [columns(ref_keys, 1 - parity), columns(ref_values, 1 - parity)], axis=1
    )
    rows = join(mine, swap(other, (Z, Z), 1), swap(other, (Z, Z), 3), swap(mine, (Z, Z), 2))
    spot = parity.astype(jnp.int32).reshape(1)
    near = [columns(a, parity) for a in (queries, grad_out)]
    far = jnp.concatenate([columns(a, 1 - parity) for a in (queries, grad_out)], axis=1)
    rows, near, far = lax.optimization_barrier((rows, near, far))
    far = swap(far, (Z, Z))
    rows = join(*gather(rows, LATE))
    blocks = gather(rows, EARLY)

    grad_queries, grad_far, *parts = attention(spot, *near, far, blocks, queries.shape)

    total = scatter_sum(parts, EARLY)
    grad_far = swap(grad_far, (Z, Z))
    total, grad_far = lax.optimization_barrier((total, grad_far))
    total = scatter_sum(jnp.split(total, 4), LATE)
    cut = jnp.split(total, 4)
    total = cut[0] + wide(swap(narrow(cut[3]), (Z, Z), 2))
    received = wide(swap(narrow(cut[1]), (Z, Z), 1)) + wide(swap(narrow(cut[2]), (Z, Z), 3))
    result, grad_queries = project(
        spot, total, received, key_weight, value_weight, grad_far, grad_queries
    )

    quarter = result.shape[1] // 4
    me = lax.axis_index("tensor")
    z_half, core = me // 2, me % 2

    def features(array, which):
        return lax.dynamic_slice_in_dim(array, which * quarter, quarter, axis=1)

    def of_core(which):
        return jnp.concatenate([features(result, which), features(result, 2 + which)], axis=1)

    pair = wide(of_core(core)) + wide(swap(of_core(1 - core), (CORE, CORE)))
    away = narrow(features(pair, 1 - z_half))
    grad_rows = features(pair, z_half) + wide(swap(away, (HALF, HALF)))
    return grad_queries, narrow(grad_rows)


def solution(mesh):
    placed = (
        P("seq", "tensor"),
        P("seq", "tensor"),
        P("seq", "tensor"),
        P("seq", "tensor"),
        P(None, "tensor"),
        P(None, "tensor"),
    )
    return jax.shard_map(
        shards,
        mesh=mesh,
        in_specs=placed,
        out_specs=(P("seq", "tensor"), P("seq", "tensor")),
        check_vma=False,
    )
```

```python
import functools
import math

import jax
import jax.numpy as jnp
from jax import lax
from jax.experimental import pallas as pl
from jax.experimental.pallas import tpu as pltpu
from jax.sharding import PartitionSpec as P

HD = 128
SCALE = 1.0 / HD**0.5
NN = (((1,), (0,)), ((), ()))
NT = (((1,), (1,)), ((), ()))
TN = (((0,), (0,)), ((), ()))

DEVICES = 256
Y, Z, X, HALF, CORE = 64, 16, 4, 2, 1
LATE = (X, Y)
EARLY = (Y, X)
STEPS = (1, 3, 2)


def swap(block, axes, step=1):
    pairs = [(i, i ^ (step * axes[i % 2])) for i in range(DEVICES)]
    return lax.ppermute(block, ("seq", "tensor"), pairs)


def gather(block, axes):
    return [block] + [swap(block, axes, step) for step in STEPS]


def scatter_sum(blocks, axes):
    total = wide(blocks[0])
    for block, step in zip(blocks[1:], STEPS):
        total += wide(swap(narrow(block), axes, step))
    return total


def wide(array):
    return array.astype(jnp.float32)


def narrow(array):
    return array.astype(jnp.bfloat16)


def dot(a, b, dims=NN):
    return lax.dot_general(a, b, dims, preferred_element_type=jnp.float32)


def join(*rows):
    return jnp.concatenate(rows, axis=0)


def attention_kernel(chunk, parity_ref, *refs):
    queries, grads_out = (refs[0], refs[2]), (refs[1], refs[3])
    keys, values = refs[4:8], refs[8:12]
    parts, grads_ref = refs[12:16], refs[16]
    rows = keys[0].shape[0]
    tokens = queries[0].shape[0]
    power = SCALE * math.log2(math.e)
    key_sums, value_sums = [0.0] * 4, [0.0] * 4

    def products(n, at):
        q, g = queries[n][pl.ds(at, chunk), :], grads_out[n][pl.ds(at, chunk), :]
        return q, g, [dot(k[...], q, NT) for k in keys], [dot(v[...], g, NT) for v in values]

    def softmax(scores, grad_probs):
        top = functools.reduce(jnp.maximum, [jnp.max(s, axis=0, keepdims=True) for s in scores])
        raised = [jnp.exp2((s - top) * power) for s in scores]
        inverse = 1.0 / sum(jnp.sum(e, axis=0, keepdims=True) for e in raised)
        probs = [e * inverse for e in raised]
        delta = sum(jnp.sum(p * d, axis=0, keepdims=True) for p, d in zip(probs, grad_probs))
        return [narrow(p) for p in probs], [
            narrow(p * (d - delta)) for p, d in zip(probs, grad_probs)
        ]

    def add(n, at, q, g, probs, grads):
        for i in range(4):
            grads_ref[pl.ds(i * rows, rows), pl.ds(n * tokens + at, chunk)] = grads[i]
            key_sums[i] += dot(grads[i], q)
            value_sums[i] += dot(probs[i], g)

    places = [(n, at) for n in range(2) for at in range(0, tokens, chunk)]
    ahead, behind = products(*places[0]), None
    for i, place in enumerate(places):
        q, g, scores, grad_probs = ahead
        if i + 1 < len(places):
            ahead = products(*places[i + 1])
        probs, grads = softmax(scores, grad_probs)
        if behind is not None:
            add(*behind)
        behind = (*place, q, g, probs, grads)
    add(*behind)
    for i in range(4):
        parts[i][:, :HD] = narrow(key_sums[i] * SCALE)
        parts[i][:, HD:] = narrow(value_sums[i])


def attention(parity, queries, grad_out, far, blocks):
    tokens = queries.shape[0]
    rows, columns = blocks[0].shape
    heads = columns // (2 * HD)
    own = pl.BlockSpec((tokens, HD), lambda h, parity: (0, h))
    first = pl.BlockSpec((tokens, HD), lambda h, parity: (0, h))
    second = pl.BlockSpec((tokens, HD), lambda h, parity: (0, heads + h))
    key = pl.BlockSpec((rows, HD), lambda h, parity: (0, h))
    value = pl.BlockSpec((rows, HD), lambda h, parity: (0, heads + h))
    part = pl.BlockSpec((rows, 2 * HD), lambda h, parity: (0, h))
    grads = pl.BlockSpec((4 * rows, 2 * tokens), lambda h, parity: (h, 0))
    scores = heads * 2 * tokens * 4 * rows
    shapes = [b.shape for b in blocks] + [(heads * 4 * rows, 2 * tokens)]
    return pl.pallas_call(
        functools.partial(attention_kernel, tokens // 4),
        grid_spec=pltpu.PrefetchScalarGridSpec(
            num_scalar_prefetch=1,
            grid=(heads,),
            in_specs=[own] * 2 + [first, second] + [key] * 4 + [value] * 4,
            out_specs=[part] * 4 + [grads],
        ),
        out_shape=[jax.ShapeDtypeStruct(shape, jnp.bfloat16) for shape in shapes],
        compiler_params=pltpu.CompilerParams(vmem_limit_bytes=24 * 2**20),
        cost_estimate=pl.CostEstimate(
            flops=8 * HD * scores,
            bytes_accessed=2 * (4 * tokens * heads * HD + 8 * rows * columns + scores),
            transcendentals=scores,
        ),
        name="attention_grads",
    )(parity, queries, grad_out, far, far, *blocks, *blocks)


def query_kernel(parity_ref, *refs):
    keys, grads_ref, near_ref, far_ref = refs[0:4], refs[4], refs[5], refs[6]
    rows = keys[0].shape[0]
    tokens = near_ref.shape[0]
    for n, out_ref in enumerate((near_ref, far_ref)):
        some = pl.ds(n * tokens, tokens)
        dq = sum(dot(k[...], grads_ref[pl.ds(i * rows, rows), some], TN) for i, k in enumerate(keys))
        out_ref[...] = narrow(dq.T * SCALE)


def query_grads(parity, blocks, grad_scores, shape):
    tokens, width = shape
    rows, columns = blocks[0].shape
    heads = columns // (2 * HD)
    return pl.pallas_call(
        query_kernel,
        grid_spec=pltpu.PrefetchScalarGridSpec(
            num_scalar_prefetch=1,
            grid=(heads,),
            in_specs=[pl.BlockSpec((rows, HD), lambda h, parity: (0, h))] * 4
            + [pl.BlockSpec((4 * rows, 2 * tokens), lambda h, parity: (h, 0))],
            out_specs=[
                pl.BlockSpec((tokens, HD), lambda h, parity: (0, parity[0] * heads + h)),
                pl.BlockSpec((tokens, HD), lambda h, parity: (0, h)),
            ],
        ),
        out_shape=[
            jax.ShapeDtypeStruct(shape, jnp.bfloat16),
            jax.ShapeDtypeStruct((tokens, heads * HD), jnp.bfloat16),
        ],
        compiler_params=pltpu.CompilerParams(vmem_limit_bytes=16 * 2**20),
        cost_estimate=pl.CostEstimate(
            flops=4 * HD * heads * tokens * 4 * rows,
            bytes_accessed=2 * heads * tokens * 8 * rows,
            transcendentals=0,
        ),
        name="query_grads",
    )(parity, *blocks, grad_scores)


def project_kernel(
    blocks,
    parity_ref,
    mine_ref,
    other_ref,
    key_ref,
    value_ref,
    far_ref,
    _,
    out_ref,
    near_ref,
    key_held,
    value_held,
    weight_sems,
    far_sem,
):
    features = key_ref.shape[0] // blocks
    copies = []
    for n in range(blocks):
        here = pl.ds(n * features, features)
        pairs = ((key_ref, key_held), (value_ref, value_held))
        copies.append(
            [
                pltpu.make_async_copy(a.at[here, :], b.at[here, :], weight_sems.at[i, n])
                for i, (a, b) in enumerate(pairs)
            ]
        )
        for copy in copies[-1]:
            copy.start()
    half = far_ref.shape[1]
    place = pl.ds(pl.multiple_of((1 - parity_ref[0]) * half, half), half)
    far_copy = pltpu.make_async_copy(far_ref, near_ref.at[:, place], far_sem)
    far_copy.start()

    def halves(sums):
        high = narrow(sums)
        return join(high, narrow(sums - wide(high)))

    rows, width = mine_ref.shape
    mine, other = halves(mine_ref[...]), halves(other_ref[...])
    first = parity_ref[0] == 0
    left = jnp.where(first, mine, other)
    right = jnp.where(first, other, mine)

    def both(start):
        picks = range(start, width, 2 * HD)
        return jnp.concatenate([a[:, at : at + HD] for a in (left, right) for at in picks], axis=1)

    keys, values = both(0), both(HD)
    for n in range(blocks):
        here = pl.ds(n * features, features)
        for copy in copies[n]:
            copy.wait()
        result = dot(keys, key_held[here, :], NT) + dot(values, value_held[here, :], NT)
        out_ref[:, here] = narrow(result[:rows] + result[rows:])
    far_copy.wait()


def project(parity, mine, other, key_weight, value_weight, grad_far, grad_queries):
    blocks = 6
    vmem = pl.BlockSpec(memory_space=pltpu.VMEM)
    whole = pl.BlockSpec(memory_space=pl.ANY)
    return pl.pallas_call(
        functools.partial(project_kernel, blocks),
        in_specs=[pl.BlockSpec(memory_space=pltpu.SMEM)] + [vmem] * 2 + [whole] * 4,
        out_specs=[vmem, whole],
        out_shape=[
            jax.ShapeDtypeStruct((mine.shape[0], key_weight.shape[0]), jnp.bfloat16),
            jax.ShapeDtypeStruct(grad_queries.shape, jnp.bfloat16),
        ],
        scratch_shapes=[pltpu.VMEM(key_weight.shape, jnp.bfloat16)] * 2
        + [pltpu.SemaphoreType.DMA((2, blocks)), pltpu.SemaphoreType.DMA],
        input_output_aliases={6: 1},
        compiler_params=pltpu.CompilerParams(vmem_limit_bytes=52 * 2**20),
        name="project_rows",
    )(parity, mine, other, key_weight, value_weight, grad_far, grad_queries)


def shards(queries, ref_keys, ref_values, grad_out, key_weight, value_weight):
    parity = lax.axis_index("seq") // (Z // X) % 2
    half = queries.shape[1] // 2

    def columns(array, which):
        return lax.dynamic_slice_in_dim(array, which * half, half, axis=1)

    mine = jnp.concatenate([columns(ref_keys, parity), columns(ref_values, parity)], axis=1)
    other = jnp.concatenate(
        [columns(ref_keys, 1 - parity), columns(ref_values, 1 - parity)], axis=1
    )
    rows = join(mine, swap(other, (Z, Z), 1), swap(other, (Z, Z), 3), swap(mine, (Z, Z), 2))
    spot = parity.astype(jnp.int32).reshape(1)
    near = [columns(a, parity) for a in (queries, grad_out)]
    far = jnp.concatenate([columns(a, 1 - parity) for a in (queries, grad_out)], axis=1)
    rows, near, far = lax.optimization_barrier((rows, near, far))
    far = swap(far, (Z, Z))
    rows = join(*gather(rows, LATE))
    blocks = gather(rows, EARLY)

    *parts, grad_scores = attention(spot, *near, far, blocks)
    grad_queries, grad_far = query_grads(spot, blocks, grad_scores, queries.shape)

    total = scatter_sum(parts, EARLY)
    grad_far = swap(grad_far, (Z, Z))
    total, grad_far = lax.optimization_barrier((total, grad_far))
    total = scatter_sum(jnp.split(total, 4), LATE)
    cut = jnp.split(total, 4)
    total = cut[0] + wide(swap(narrow(cut[3]), (Z, Z), 2))
    received = wide(swap(narrow(cut[1]), (Z, Z), 1)) + wide(swap(narrow(cut[2]), (Z, Z), 3))
    result, grad_queries = project(
        spot, total, received, key_weight, value_weight, grad_far, grad_queries
    )

    quarter = result.shape[1] // 4
    me = lax.axis_index("tensor")
    z_half, core = me // 2, me % 2

    def features(array, which):
        return lax.dynamic_slice_in_dim(array, which * quarter, quarter, axis=1)

    def of_core(which):
        return jnp.concatenate([features(result, which), features(result, 2 + which)], axis=1)

    pair = wide(of_core(core)) + wide(swap(of_core(1 - core), (CORE, CORE)))
    away = narrow(features(pair, 1 - z_half))
    grad_rows = features(pair, z_half) + wide(swap(away, (HALF, HALF)))
    return grad_queries, narrow(grad_rows)


def solution(mesh):
    placed = (
        P("seq", "tensor"),
        P("seq", "tensor"),
        P("seq", "tensor"),
        P("seq", "tensor"),
        P(None, "tensor"),
        P(None, "tensor"),
    )
    return jax.shard_map(
        shards,
        mesh=mesh,
        in_specs=placed,
        out_specs=(P("seq", "tensor"), P("seq", "tensor")),
        check_vma=False,
    )
```

```python
import functools
import math

import jax
import jax.numpy as jnp
from jax import lax
from jax.experimental import pallas as pl
from jax.experimental.pallas import tpu as pltpu
from jax.sharding import PartitionSpec as P

HD = 128
SCALE = 1.0 / HD**0.5
NN = (((1,), (0,)), ((), ()))
NT = (((1,), (1,)), ((), ()))
TN = (((0,), (0,)), ((), ()))

DEVICES = 256
Y, Z, X, HALF, CORE = 64, 16, 4, 2, 1
LATE = (X, Y)
EARLY = (Y, X)
STEPS = (1, 3, 2)


def swap(block, axes, step=1):
    pairs = [(i, i ^ (step * axes[i % 2])) for i in range(DEVICES)]
    return lax.ppermute(block, ("seq", "tensor"), pairs)


def gather(block, axes):
    return [block] + [swap(block, axes, step) for step in STEPS]


def scatter_sum(blocks, axes):
    total = wide(blocks[0])
    for block, step in zip(blocks[1:], STEPS):
        total += wide(swap(narrow(block), axes, step))
    return total


def wide(array):
    return array.astype(jnp.float32)


def narrow(array):
    return array.astype(jnp.bfloat16)


def dot(a, b, dims=NN):
    return lax.dot_general(a, b, dims, preferred_element_type=jnp.float32)


def join(*rows):
    return jnp.concatenate(rows, axis=0)


def attention_kernel(chunk, parity_ref, *refs):
    queries, grads_out = (refs[0], refs[2]), (refs[1], refs[3])
    keys, values = refs[4:8], refs[8:12]
    parts, grads_ref, probs_ref = refs[12:15], refs[15], refs[16]
    rows = keys[0].shape[0]
    tokens = queries[0].shape[0]
    power = SCALE * math.log2(math.e)
    key_sums, value_sums = [0.0] * 4, [0.0] * 4

    def products(n, at):
        q, g = queries[n][pl.ds(at, chunk), :], grads_out[n][pl.ds(at, chunk), :]
        return q, g, [dot(k[...], q, NT) for k in keys], [dot(v[...], g, NT) for v in values]

    def softmax(scores, grad_probs):
        top = functools.reduce(jnp.maximum, [jnp.max(s, axis=0, keepdims=True) for s in scores])
        raised = [jnp.exp2((s - top) * power) for s in scores]
        inverse = 1.0 / sum(jnp.sum(e, axis=0, keepdims=True) for e in raised)
        probs = [e * inverse for e in raised]
        delta = sum(jnp.sum(p * d, axis=0, keepdims=True) for p, d in zip(probs, grad_probs))
        return [narrow(p) for p in probs], [
            narrow(p * (d - delta)) for p, d in zip(probs, grad_probs)
        ]

    def add(n, at, q, g, probs, grads):
        probs_ref[:, pl.ds(n * tokens + at, chunk)] = probs[0]
        for i in range(4):
            grads_ref[pl.ds(i * rows, rows), pl.ds(n * tokens + at, chunk)] = grads[i]
        for i in range(1, 4):
            key_sums[i] += dot(grads[i], q)
            value_sums[i] += dot(probs[i], g)

    places = [(n, at) for n in range(2) for at in range(0, tokens, chunk)]
    ahead, behind = products(*places[0]), None
    for i, place in enumerate(places):
        q, g, scores, grad_probs = ahead
        if i + 1 < len(places):
            ahead = products(*places[i + 1])
        probs, grads = softmax(scores, grad_probs)
        if behind is not None:
            add(*behind)
        behind = (*place, q, g, probs, grads)
    add(*behind)
    for i in range(1, 4):
        parts[i - 1][:, :HD] = narrow(key_sums[i] * SCALE)
        parts[i - 1][:, HD:] = narrow(value_sums[i])


def attention(parity, queries, grad_out, far, blocks):
    tokens = queries.shape[0]
    rows, columns = blocks[0].shape
    heads = columns // (2 * HD)
    own = pl.BlockSpec((tokens, HD), lambda h, parity: (0, h))
    first = pl.BlockSpec((tokens, HD), lambda h, parity: (0, h))
    second = pl.BlockSpec((tokens, HD), lambda h, parity: (0, heads + h))
    key = pl.BlockSpec((rows, HD), lambda h, parity: (0, h))
    value = pl.BlockSpec((rows, HD), lambda h, parity: (0, heads + h))
    part = pl.BlockSpec((rows, 2 * HD), lambda h, parity: (0, h))
    grads = pl.BlockSpec((4 * rows, 2 * tokens), lambda h, parity: (h, 0))
    probs = pl.BlockSpec((rows, 2 * tokens), lambda h, parity: (h, 0))
    scores = heads * 2 * tokens * 4 * rows
    shapes = [b.shape for b in blocks[1:]]
    shapes += [(heads * n * rows, 2 * tokens) for n in (4, 1)]
    return pl.pallas_call(
        functools.partial(attention_kernel, tokens // 4),
        grid_spec=pltpu.PrefetchScalarGridSpec(
            num_scalar_prefetch=1,
            grid=(heads,),
            in_specs=[own] * 2 + [first, second] + [key] * 4 + [value] * 4,
            out_specs=[part] * 3 + [grads, probs],
        ),
        out_shape=[jax.ShapeDtypeStruct(shape, jnp.bfloat16) for shape in shapes],
        compiler_params=pltpu.CompilerParams(vmem_limit_bytes=24 * 2**20),
        cost_estimate=pl.CostEstimate(
            flops=8 * HD * scores,
            bytes_accessed=2 * (4 * tokens * heads * HD + 8 * rows * columns + scores),
            transcendentals=scores,
        ),
        name="attention_grads",
    )(parity, queries, grad_out, far, far, *blocks, *blocks)


def query_kernel(parity_ref, *refs):
    keys, grads_ref, probs_ref = refs[0:4], refs[4], refs[5]
    queries, grads_out = (refs[6], refs[8]), (refs[7], refs[9])
    near_ref, far_ref, own_ref = refs[10:]
    rows = keys[0].shape[0]
    tokens = near_ref.shape[0]
    for n, out_ref in enumerate((near_ref, far_ref)):
        some = pl.ds(n * tokens, tokens)
        dq = sum(dot(k[...], grads_ref[pl.ds(i * rows, rows), some], TN) for i, k in enumerate(keys))
        out_ref[...] = narrow(dq.T * SCALE)
    spans = [pl.ds(n * tokens, tokens) for n in range(2)]
    dk = sum(dot(grads_ref[pl.ds(0, rows), t], q[...]) for t, q in zip(spans, queries))
    own_ref[:, :HD] = dk * SCALE
    own_ref[:, HD:] = sum(dot(probs_ref[:, t], g[...]) for t, g in zip(spans, grads_out))


def query_grads(parity, blocks, grad_scores, probs, queries, grad_out, far, shape):
    tokens, width = shape
    rows, columns = blocks[0].shape
    heads = columns // (2 * HD)
    return pl.pallas_call(
        query_kernel,
        grid_spec=pltpu.PrefetchScalarGridSpec(
            num_scalar_prefetch=1,
            grid=(heads,),
            in_specs=[pl.BlockSpec((rows, HD), lambda h, parity: (0, h))] * 4
            + [pl.BlockSpec((n * rows, 2 * tokens), lambda h, parity: (h, 0)) for n in (4, 1)]
            + [pl.BlockSpec((tokens, HD), lambda h, parity: (0, h))] * 3
            + [pl.BlockSpec((tokens, HD), lambda h, parity: (0, heads + h))],
            out_specs=[
                pl.BlockSpec((tokens, HD), lambda h, parity: (0, parity[0] * heads + h)),
                pl.BlockSpec((tokens, HD), lambda h, parity: (0, h)),
                pl.BlockSpec((rows, 2 * HD), lambda h, parity: (0, h)),
            ],
        ),
        out_shape=[
            jax.ShapeDtypeStruct(shape, jnp.bfloat16),
            jax.ShapeDtypeStruct((tokens, heads * HD), jnp.bfloat16),
            jax.ShapeDtypeStruct((rows, columns), jnp.float32),
        ],
        compiler_params=pltpu.CompilerParams(vmem_limit_bytes=16 * 2**20),
        cost_estimate=pl.CostEstimate(
            flops=4 * HD * heads * tokens * 4 * rows,
            bytes_accessed=2 * heads * tokens * 8 * rows,
            transcendentals=0,
        ),
        name="query_grads",
    )(parity, *blocks, grad_scores, probs, queries, grad_out, far, far)


def project_kernel(
    blocks,
    parity_ref,
    mine_ref,
    other_ref,
    key_ref,
    value_ref,
    far_ref,
    _,
    out_ref,
    near_ref,
    key_held,
    value_held,
    weight_sems,
    far_sem,
):
    features = key_ref.shape[0] // blocks
    copies = []
    for n in range(blocks):
        here = pl.ds(n * features, features)
        pairs = ((key_ref, key_held), (value_ref, value_held))
        copies.append(
            [
                pltpu.make_async_copy(a.at[here, :], b.at[here, :], weight_sems.at[i, n])
                for i, (a, b) in enumerate(pairs)
            ]
        )
        for copy in copies[-1]:
            copy.start()
    half = far_ref.shape[1]
    place = pl.ds(pl.multiple_of((1 - parity_ref[0]) * half, half), half)
    far_copy = pltpu.make_async_copy(far_ref, near_ref.at[:, place], far_sem)
    far_copy.start()

    def halves(sums):
        high = narrow(sums)
        return join(high, narrow(sums - wide(high)))

    rows, width = mine_ref.shape
    mine, other = halves(mine_ref[...]), halves(other_ref[...])
    first = parity_ref[0] == 0
    left = jnp.where(first, mine, other)
    right = jnp.where(first, other, mine)

    def both(start):
        picks = range(start, width, 2 * HD)
        return jnp.concatenate([a[:, at : at + HD] for a in (left, right) for at in picks], axis=1)

    keys, values = both(0), both(HD)
    for n in range(blocks):
        here = pl.ds(n * features, features)
        for copy in copies[n]:
            copy.wait()
        result = dot(keys, key_held[here, :], NT) + dot(values, value_held[here, :], NT)
        out_ref[:, here] = narrow(result[:rows] + result[rows:])
    far_copy.wait()


def project(parity, mine, other, key_weight, value_weight, grad_far, grad_queries):
    blocks = 6
    vmem = pl.BlockSpec(memory_space=pltpu.VMEM)
    whole = pl.BlockSpec(memory_space=pl.ANY)
    return pl.pallas_call(
        functools.partial(project_kernel, blocks),
        in_specs=[pl.BlockSpec(memory_space=pltpu.SMEM)] + [vmem] * 2 + [whole] * 4,
        out_specs=[vmem, whole],
        out_shape=[
            jax.ShapeDtypeStruct((mine.shape[0], key_weight.shape[0]), jnp.bfloat16),
            jax.ShapeDtypeStruct(grad_queries.shape, jnp.bfloat16),
        ],
        scratch_shapes=[pltpu.VMEM(key_weight.shape, jnp.bfloat16)] * 2
        + [pltpu.SemaphoreType.DMA((2, blocks)), pltpu.SemaphoreType.DMA],
        input_output_aliases={6: 1},
        compiler_params=pltpu.CompilerParams(vmem_limit_bytes=52 * 2**20),
        name="project_rows",
    )(parity, mine, other, key_weight, value_weight, grad_far, grad_queries)


def shards(queries, ref_keys, ref_values, grad_out, key_weight, value_weight):
    parity = lax.axis_index("seq") // (Z // X) % 2
    half = queries.shape[1] // 2

    def columns(array, which):
        return lax.dynamic_slice_in_dim(array, which * half, half, axis=1)

    mine = jnp.concatenate([columns(ref_keys, parity), columns(ref_values, parity)], axis=1)
    other = jnp.concatenate(
        [columns(ref_keys, 1 - parity), columns(ref_values, 1 - parity)], axis=1
    )
    rows = join(mine, swap(other, (Z, Z), 1), swap(other, (Z, Z), 3), swap(mine, (Z, Z), 2))
    spot = parity.astype(jnp.int32).reshape(1)
    near = [columns(a, parity) for a in (queries, grad_out)]
    far = jnp.concatenate([columns(a, 1 - parity) for a in (queries, grad_out)], axis=1)
    rows, near, far = lax.optimization_barrier((rows, near, far))
    far = swap(far, (Z, Z))
    rows = join(*gather(rows, LATE))
    blocks = gather(rows, EARLY)

    *parts, grad_scores, probs = attention(spot, *near, far, blocks)
    grad_queries, grad_far, own = query_grads(
        spot, blocks, grad_scores, probs, *near, far, queries.shape
    )

    total = scatter_sum([own, *parts], EARLY)
    grad_far = swap(grad_far, (Z, Z))
    total, grad_far = lax.optimization_barrier((total, grad_far))
    total = scatter_sum(jnp.split(total, 4), LATE)
    cut = jnp.split(total, 4)
    total = cut[0] + wide(swap(narrow(cut[3]), (Z, Z), 2))
    received = wide(swap(narrow(cut[1]), (Z, Z), 1)) + wide(swap(narrow(cut[2]), (Z, Z), 3))
    result, grad_queries = project(
        spot, total, received, key_weight, value_weight, grad_far, grad_queries
    )

    quarter = result.shape[1] // 4
    me = lax.axis_index("tensor")
    z_half, core = me // 2, me % 2

    def features(array, which):
        return lax.dynamic_slice_in_dim(array, which * quarter, quarter, axis=1)

    def of_core(which):
        return jnp.concatenate([features(result, which), features(result, 2 + which)], axis=1)

    pair = wide(of_core(core)) + wide(swap(of_core(1 - core), (CORE, CORE)))
    away = narrow(features(pair, 1 - z_half))
    grad_rows = features(pair, z_half) + wide(swap(away, (HALF, HALF)))
    return grad_queries, narrow(grad_rows)


def solution(mesh):
    placed = (
        P("seq", "tensor"),
        P("seq", "tensor"),
        P("seq", "tensor"),
        P("seq", "tensor"),
        P(None, "tensor"),
        P(None, "tensor"),
    )
    return jax.shard_map(
        shards,
        mesh=mesh,
        in_specs=placed,
        out_specs=(P("seq", "tensor"), P("seq", "tensor")),
        check_vma=False,
    )
```
